128 devices in a mesh: ctx: 16 (over z_lo, y, core), head: 8 (over z_hi, x).
Axes of the slice: x: 4, y: 4, z: 4 (z_hi: 2, z_lo: 2; z = z_hi * 2 + z_lo), core: 2. Of those that a mesh axis runs over, the one named last changes fastest.
Arguments:
- tokens: bfloat16 [8192, 8192], P('ctx'), may hold values from -210 to 210
- positions: int32 [8192], P('ctx'), may hold values from 0 to 8191, each once
- stored_qkv: bfloat16 [8192, 6144], P(('ctx', 'head')), may hold values from -0.109375 to 0.109375
- block_order: int32 [64], replicated, may hold values from 0 to 63, each once
- qkv_bias: float32 [6144], P('head'), may hold values from -3 to 3
Outputs:
- attended: bfloat16 [8192, 4096], P('ctx', 'head')
The draws below stay inside these ranges and needn't reach their ends.
Inputs may be any that keep to these rules, and one draw needn't show every extreme that they name: `positions`: each position of 0 to 8191 appears once. `block_order`: each row block appears once.
All inputs are finite; a program needn't handle non-finite values.
Results may differ from the reference program's by a relative error of at most 0.04.
Values may be sent and summed in bfloat16 or wider, within the bound.
No kernel may reach another device: no remote copies, remote signals or barrier semaphores. Data moves between devices by JAX's collectives and lax.ppermute only.
A program may use at most 128 MiB of HBM per device.

```python
import math
import jax
import jax.numpy as jnp
from jax import lax

D = 8192
HEAD_DIM = 128
QPG = 4
ROW_BLOCK = 128
TOKENS = 8192
KV_HEADS = 8
COLUMNS = 6144


def draw_tokens(key, part):
    key = jax.random.fold_in(key, 7)
    first = jax.random.fold_in(key, 0)
    base = jnp.clip(jax.random.normal(first, (TOKENS, D), jnp.float32), -6.0, 6.0)
    return base.astype(jnp.bfloat16)


def shard_levels(stream_key, shape, shards, smallest, top_value):
    loudness, own = 1.0, jax.random.fold_in(stream_key, 6)
    for position, blocks in shards:
        heights = jnp.exp(jax.random.uniform(jax.random.fold_in(own, position), (blocks,), jnp.float32, smallest / len(shards), top_value / len(shards)))
        loudness = loudness * jnp.repeat(heights, shape[position] // blocks).reshape([-1 if axis == position else 1 for axis in range(len(shape))])
    return loudness


def normal_values(key, dims, deviation, limit, shards=(), kind=jnp.bfloat16):
    level = shard_levels(key, dims, shards, -0.22, 0.18) if shards else 1.0
    values = jax.random.normal(key, dims, jnp.float32) * deviation * level
    return jnp.minimum(jnp.maximum(values, -limit), limit).astype(kind)


def setup_inputs(seed: int = 0) -> dict:
    key_of = jax.random.split(jax.random.key(seed), 6)
    return {
        "tokens": draw_tokens(jax.random.fold_in(key_of[5], 71), 0),
        "positions": jax.random.permutation(key_of[1], TOKENS).astype(jnp.int32),
        "stored_qkv": normal_values(key_of[2], (D, COLUMNS), (D // 3) ** -0.5, 0.109375, ((0, 128),)),
        "block_order": jax.random.permutation(key_of[3], D // ROW_BLOCK).astype(jnp.int32),
        "qkv_bias": normal_values(key_of[4], (COLUMNS,), 0.5, 3.0, ((0, 8),), jnp.float32),
    }


theta_base = 1000000.0

def angles(positions, width):
    half = width // 2
    freq = jnp.exp(jnp.arange(half, dtype=jnp.float32) * (-2.0 * math.log(theta_base) / width))
    phase = positions.astype(jnp.float32)[:, None] * freq[None, :]
    return (jnp.cos(phase), jnp.sin(phase))

def rotate(values, cosine, sine):
    half = values.shape[-1] // 2
    first = values[..., :half]
    second = values[..., half:]
    return jnp.concatenate([first * cosine - second * sine, second * cosine + first * sine], axis=-1)

def reference(tokens, positions, stored_qkv, block_order, qkv_bias):
    blocks = D // ROW_BLOCK
    inverse = jnp.argsort(block_order).astype(jnp.int32)
    weight = stored_qkv.reshape(blocks, ROW_BLOCK, COLUMNS)[inverse].reshape(D, COLUMNS)
    qkv = jnp.dot(tokens, weight, preferred_element_type=jnp.float32) + qkv_bias[None, :]
    qkv = qkv.reshape(TOKENS, KV_HEADS, QPG + 2, HEAD_DIM)
    cosine, sine = angles(positions, HEAD_DIM)
    turned = rotate(qkv[:, :, :QPG + 1], cosine[:, None, None, :], sine[:, None, None, :])
    queries = turned[:, :, :QPG].astype(jnp.bfloat16)
    keys = turned[:, :, QPG].astype(jnp.bfloat16)
    values = qkv[:, :, QPG + 1].astype(jnp.bfloat16)
    scale = 1.0 / math.sqrt(HEAD_DIM)
    rows = math.gcd(TOKENS, 512)

    def one_group(items):
        group_q, group_k, group_v = items
        key_f = group_k.astype(jnp.float32)
        value_f = group_v.astype(jnp.float32)

        def one_block(start):
            query = lax.dynamic_slice_in_dim(group_q, start, rows, 0).astype(jnp.float32)
            query_pos = lax.dynamic_slice_in_dim(positions, start, rows, 0)
            score = jnp.einsum('rhd,kd->hrk', query, key_f) * scale
            allowed = positions[None, None, :] <= query_pos[None, :, None]
            score = jnp.where(allowed, score, -1e+30)
            top = lax.optimization_barrier(jnp.max(score, axis=-1, keepdims=True))
            prob = jnp.where(allowed, jnp.exp(score - top), 0.0)
            total = lax.optimization_barrier(jnp.sum(prob, axis=-1))
            rounded = lax.optimization_barrier(prob.astype(jnp.bfloat16)).astype(jnp.float32)
            numer = jnp.einsum('hrk,kd->hrd', rounded, value_f)
            result = numer / total[..., None]
            return jnp.transpose(result, (1, 0, 2)).reshape(rows, QPG * HEAD_DIM)
        starts = jnp.arange(TOKENS // rows, dtype=jnp.int32) * rows
        return lax.map(one_block, starts).reshape(TOKENS, QPG * HEAD_DIM)
    outputs = lax.map(one_group, (jnp.transpose(queries, (1, 0, 2, 3)), jnp.transpose(keys, (1, 0, 2)), jnp.transpose(values, (1, 0, 2))))
    return jnp.transpose(outputs, (1, 0, 2)).reshape(TOKENS, KV_HEADS * QPG * HEAD_DIM).astype(jnp.bfloat16)
```

```python
import math

import jax
import jax.numpy as jnp
from jax import lax
from jax.experimental import pallas as pl
from jax.experimental.pallas import tpu as pltpu
from jax.sharding import Mesh
from jax.sharding import PartitionSpec as P

HEAD_DIM = 128
QPG = 4
theta_base = 1000000.0

SIZES = {"zl": 2, "y": 4, "core": 2, "zh": 2, "x": 4}
CTX = ("zl", "y", "core")
HEAD = ("zh", "x")
OFFSETS = ((0, 0), (1, 0), (0, -1), (0, 1), (0, 2), (1, -1), (1, 1), (1, 2))
PIECES = len(OFFSETS)
MIB = 1024 * 1024


def shift(block, axis, distance):
    size = SIZES[axis]
    return lax.ppermute(block, axis, [(i, (i + distance) % size) for i in range(size)])


def spread(block):
    over = shift(block, "zl", 1)
    left = shift(block, "y", 1)
    right = shift(block, "y", -1)
    far = shift(block, "y", 2)
    return (
        block, over, left, right, far,
        shift(over, "y", 1), shift(over, "y", -1), shift(far, "zl", 1),
    )


def arrange_kernel(cols_ref, order_ref, a_ref, b_ref, c_ref, d_ref, out_ref):
    block = jnp.concatenate([a_ref[...], b_ref[...], c_ref[...], d_ref[...]], axis=1)
    out_ref[0] = jnp.dot(order_ref[...], block, preferred_element_type=jnp.float32).astype(
        out_ref.dtype
    )


def arrange(tokens, order, cols):
    rows, width = tokens.shape
    part = 128

    def pick(j):
        return pl.BlockSpec((rows, part), lambda p, cols_ref: (0, cols_ref[4 * p + j]))

    return pl.pallas_call(
        arrange_kernel,
        grid_spec=pltpu.PrefetchScalarGridSpec(
            num_scalar_prefetch=1,
            grid=(PIECES,),
            in_specs=[pl.BlockSpec((rows, rows), lambda p, cols_ref: (0, 0))]
            + [pick(j) for j in range(4)],
            out_specs=pl.BlockSpec((1, rows, 4 * part), lambda p, cols_ref: (p, 0, 0)),
        ),
        out_shape=jax.ShapeDtypeStruct((PIECES, rows, 4 * part), jnp.bfloat16),
        compiler_params=pltpu.CompilerParams(vmem_limit_bytes=32 * MIB),
        cost_estimate=pl.CostEstimate(
            flops=2 * rows * rows * width // 2, bytes_accessed=2 * rows * width, transcendentals=0
        ),
        name="arrange",
    )(cols, order, tokens, tokens, tokens, tokens)


def project_kernel(*refs):
    x_own, x_sib = refs[0], refs[1]
    pieces = refs[2 : 2 + PIECES]
    out_own, out_sib = refs[2 + PIECES], refs[3 + PIECES]
    x_buf, w_buf, sems = refs[4 + PIECES :]
    copies = []
    for p in range(PIECES):
        group = (
            pltpu.make_async_copy(pieces[p], w_buf.at[p], sems.at[0, p]),
            pltpu.make_async_copy(x_own.at[p], x_buf.at[0, p], sems.at[1, p]),
            pltpu.make_async_copy(x_sib.at[p], x_buf.at[1, p], sems.at[2, p]),
        )
        for copy in group:
            copy.start()
        copies.append(group)
    for p in range(PIECES):
        for copy in copies[p]:
            copy.wait()
        for half, out in enumerate((out_own, out_sib)):
            term = jnp.dot(x_buf[half, p], w_buf[p], preferred_element_type=jnp.float32)
            if p == 0:
                out[...] = term
            else:
                out[...] += term


def project(x_own, x_sib, pieces):
    rows = x_own.shape[1]
    depth, width = pieces[0].shape
    out = jax.ShapeDtypeStruct((rows, width), jnp.float32)
    return pl.pallas_call(
        project_kernel,
        in_specs=[pl.BlockSpec(memory_space=pl.ANY)] * (2 + PIECES),
        out_specs=[pl.BlockSpec(memory_space=pltpu.VMEM)] * 2,
        out_shape=[out, out],
        scratch_shapes=[
            pltpu.VMEM((2, PIECES, rows, depth), jnp.bfloat16),
            pltpu.VMEM((PIECES, depth, width), jnp.bfloat16),
            pltpu.SemaphoreType.DMA((3, PIECES)),
        ],
        compiler_params=pltpu.CompilerParams(vmem_limit_bytes=48 * MIB),
        cost_estimate=pl.CostEstimate(
            flops=4 * rows * width * depth * PIECES,
            bytes_accessed=PIECES * depth * (4 * rows + 2 * width),
            transcendentals=0,
        ),
        name="project",
    )(x_own, x_sib, *pieces)


def turn_kernel(scale, mine_ref, other_ref, bias_ref, cos_ref, sin_ref, q_ref, kv_ref):
    both = mine_ref[...] + other_ref[...] + bias_ref[...]
    cosine, sine = cos_ref[...], sin_ref[...]
    half = HEAD_DIM // 2
    for head in range(QPG + 1):
        x = both[:, head * HEAD_DIM : (head + 1) * HEAD_DIM]
        swapped = jnp.concatenate([x[:, half:], x[:, :half]], axis=1)
        y = x * cosine + swapped * sine
        if head < QPG:
            q_ref[:, head * HEAD_DIM : (head + 1) * HEAD_DIM] = (y * scale).astype(q_ref.dtype)
        else:
            kv_ref[:, :HEAD_DIM] = y.astype(kv_ref.dtype)
    kv_ref[:, HEAD_DIM:] = both[:, (QPG + 1) * HEAD_DIM :].astype(kv_ref.dtype)


def turn(mine, other, bias, cosine, sine):
    rows, width = mine.shape
    scale = math.log2(math.e) / math.sqrt(HEAD_DIM)
    return pl.pallas_call(
        lambda *refs: turn_kernel(scale, *refs),
        grid=(4,),
        in_specs=[
            pl.BlockSpec((rows // 4, width), lambda i: (i, 0)),
            pl.BlockSpec((rows // 4, width), lambda i: (i, 0)),
            pl.BlockSpec((1, width), lambda i: (0, 0)),
            pl.BlockSpec((rows // 4, HEAD_DIM), lambda i: (i, 0)),
            pl.BlockSpec((rows // 4, HEAD_DIM), lambda i: (i, 0)),
        ],
        out_specs=[
            pl.BlockSpec((rows // 4, QPG * HEAD_DIM), lambda i: (i, 0)),
            pl.BlockSpec((rows // 4, 2 * HEAD_DIM), lambda i: (i, 0)),
        ],
        out_shape=[
            jax.ShapeDtypeStruct((rows, QPG * HEAD_DIM), jnp.bfloat16),
            jax.ShapeDtypeStruct((rows, 2 * HEAD_DIM), jnp.bfloat16),
        ],
        cost_estimate=pl.CostEstimate(
            flops=4 * rows * width, bytes_accessed=10 * rows * width, transcendentals=0
        ),
        name="turn",
    )(mine, other, bias, cosine, sine)


STRIP = 64
KV_PIECES = 2 * PIECES
KEY_TILE = STRIP * KV_PIECES


def attend_kernel(full_ref, some_ref, q_ref, qpos_ref, kpos_ref, back_ref, *refs):
    pieces = refs[:KV_PIECES]
    out_ref, gathered = refs[KV_PIECES:]
    i = pl.program_id(0)
    q = jnp.concatenate(
        [q_ref[:, h * HEAD_DIM : (h + 1) * HEAD_DIM] for h in range(QPG)], axis=0
    )
    qpos = jnp.concatenate([qpos_ref[...]] * QPG, axis=0)
    ones = jnp.ones((KEY_TILE, HEAD_DIM), jnp.bfloat16)

    def absorb(masked, t, state):
        best, accum = state
        row = pl.ds(pl.multiple_of(t * STRIP, STRIP), STRIP)
        keys = jnp.concatenate([p[row, :HEAD_DIM] for p in pieces], axis=0)
        values = jnp.concatenate([p[row, HEAD_DIM:] for p in pieces], axis=0)
        values = jnp.concatenate([values, ones], axis=1)
        score = lax.dot_general(
            q, keys, (((1,), (1,)), ((), ())), preferred_element_type=jnp.float32
        )
        if masked:
            score = jnp.where(kpos_ref[t] <= qpos, score, -1e30)
        newest = jnp.maximum(best, jnp.max(score, axis=1, keepdims=True))
        prob = jnp.exp2((score - newest).astype(jnp.bfloat16))
        accum = accum * jnp.exp2(best - newest) + jnp.dot(
            prob, values, preferred_element_type=jnp.float32
        )
        return newest, accum

    state = (
        jnp.full((QPG * STRIP, 1), -1e30, jnp.float32),
        jnp.zeros((QPG * STRIP, 2 * HEAD_DIM), jnp.float32),
    )
    state = lax.fori_loop(0, full_ref[i], lambda t, s: absorb(False, t, s), state)
    _, accum = lax.fori_loop(full_ref[i], some_ref[i], lambda t, s: absorb(True, t, s), state)
    result = (accum[:, :HEAD_DIM] / accum[:, HEAD_DIM:]).astype(jnp.bfloat16)
    rows = pl.ds(pl.multiple_of(i * STRIP, STRIP), STRIP)
    for h in range(QPG):
        gathered[rows, h * HEAD_DIM : (h + 1) * HEAD_DIM] = result[h * STRIP : (h + 1) * STRIP]

    @pl.when(i == pl.num_programs(0) - 1)
    def _():
        out_ref[...] = jnp.dot(
            back_ref[...], gathered[...], preferred_element_type=jnp.float32
        ).astype(out_ref.dtype)


def attend(full, some, q, qpos, kpos, back, pieces):
    rows, width = q.shape
    tiles = kpos.shape[0]
    return pl.pallas_call(
        attend_kernel,
        grid_spec=pltpu.PrefetchScalarGridSpec(
            num_scalar_prefetch=2,
            grid=(rows // STRIP,),
            in_specs=[
                pl.BlockSpec((STRIP, width), lambda i, *_: (i, 0)),
                pl.BlockSpec((STRIP, 1), lambda i, *_: (i, 0)),
                pl.BlockSpec((tiles, 1, KEY_TILE), lambda i, *_: (0, 0, 0)),
                pl.BlockSpec((rows, rows), lambda i, *_: (0, 0)),
            ]
            + [pl.BlockSpec((rows, 2 * HEAD_DIM), lambda i, *_: (0, 0))] * KV_PIECES,
            out_specs=pl.BlockSpec((rows, width), lambda i, *_: (0, 0)),
            scratch_shapes=[pltpu.VMEM((rows, width), jnp.bfloat16)],
        ),
        out_shape=jax.ShapeDtypeStruct((rows, width), jnp.bfloat16),
        compiler_params=pltpu.CompilerParams(vmem_limit_bytes=48 * MIB),
        cost_estimate=pl.CostEstimate(
            flops=4 * rows * width * tiles * KEY_TILE // 2,
            bytes_accessed=4 * rows * KV_PIECES * HEAD_DIM,
            transcendentals=rows * QPG * tiles * KEY_TILE // 2,
        ),
        name="attend",
    )(full, some, q, qpos, kpos, back, *pieces)


def angles(positions, width):
    half = width // 2
    freq = jnp.exp(jnp.arange(half, dtype=jnp.float32) * (-2.0 * math.log(theta_base) / width))
    phase = positions.astype(jnp.float32)[:, None] * freq[None, :]
    return (jnp.cos(phase), jnp.sin(phase))


def local(tokens, positions, stored_qkv, block_order, qkv_bias):
    rows = tokens.shape[0]
    zl, y, core = (lax.axis_index(a) for a in CTX)

    rank = jnp.sum(positions[None, :] < positions[:, None], axis=1, dtype=jnp.int32)
    chosen = rank[None, :] == jnp.arange(rows, dtype=jnp.int32)[:, None]
    order = chosen.astype(jnp.bfloat16)
    back = (rank[:, None] == jnp.arange(rows, dtype=jnp.int32)[None, :]).astype(jnp.bfloat16)
    place = jnp.sum(jnp.where(chosen, positions[None, :], 0), axis=1, dtype=jnp.int32)

    def owners(which):
        return jnp.stack([(((zl + a) % 2) * 4 + (y + b) % 4) * 2 + which for a, b in OFFSETS])

    def columns(which):
        blocks = owners(which)[:, None] * 4 + jnp.arange(4, dtype=jnp.int32)[None, :]
        return block_order[blocks.reshape(-1)]

    x_away = arrange(tokens, order, columns(1 - core))
    x_sib = shift(x_away, "core", 1)
    x_own = arrange(tokens, order, columns(core))

    mine = lax.all_to_all(stored_qkv, HEAD, split_axis=1, concat_axis=0, tiled=True)
    own, away = project(x_own, x_sib, spread(mine))
    other = shift(away, "core", 1)

    cosine, sine = angles(place, HEAD_DIM)
    q, kv = turn(
        own, other, qkv_bias[None, :],
        jnp.concatenate([cosine, cosine], axis=1), jnp.concatenate([-sine, sine], axis=1),
    )

    near = spread(kv)
    pieces = near + tuple(shift(block, "core", 1) for block in near)

    every = lax.all_gather(place, CTX, axis=0, tiled=False)
    kpos = every[jnp.concatenate([owners(core), owners(1 - core)])]
    tiles = rows // STRIP
    kpos = kpos.reshape(KV_PIECES, tiles, STRIP).transpose(1, 0, 2).reshape(tiles, KEY_TILE)
    low, high = jnp.min(kpos, axis=1), jnp.max(kpos, axis=1)
    strips = place.reshape(rows // STRIP, STRIP)
    full = jnp.sum(high[None, :] <= strips[:, :1], axis=1, dtype=jnp.int32)
    some = jnp.sum(low[None, :] <= strips[:, -1:], axis=1, dtype=jnp.int32)
    return attend(full, some, q, place[:, None], kpos[:, None, :], back, pieces)


def solution(mesh):
    fine = Mesh(mesh.devices.reshape(tuple(SIZES.values())), tuple(SIZES))
    placed = (P(CTX, None), P(CTX), P(CTX + HEAD, None), P(), P(HEAD))
    return jax.shard_map(
        local, mesh=fine, in_specs=placed, out_specs=P(CTX, HEAD), check_vma=False
    )
```

```python
import functools
import math

import jax
import jax.numpy as jnp
from jax import lax
from jax.experimental import pallas as pl
from jax.experimental.pallas import tpu as pltpu
from jax.sharding import Mesh
from jax.sharding import PartitionSpec as P

HEAD_DIM = 128
QPG = 4
theta_base = 1000000.0

SIZES = {"zl": 2, "y": 4, "core": 2, "zh": 2, "x": 4}
CTX = ("zl", "y", "core")
HEAD = ("zh", "x")
OFFSETS = ((0, 0), (1, 0), (0, -1), (0, 1), (0, 2), (1, -1), (1, 1), (1, 2))
PIECES = len(OFFSETS)
MIB = 1024 * 1024
SMALL = pl.CostEstimate(flops=1, bytes_accessed=1, transcendentals=0)


def shift(block, axis, distance):
    size = SIZES[axis]
    return lax.ppermute(block, axis, [(i, (i + distance) % size) for i in range(size)])


def second(over, far):
    return far, shift(over, "y", 1), shift(over, "y", -1), shift(far, "zl", 1)


def after_kernel(*refs):
    del refs


def after(arrays, *tokens):
    count = len(arrays)
    return pl.pallas_call(
        after_kernel,
        in_specs=[pl.BlockSpec(memory_space=pl.ANY)] * (count + len(tokens)),
        out_specs=[pl.BlockSpec(memory_space=pl.ANY)] * count,
        out_shape=[jax.ShapeDtypeStruct(a.shape, a.dtype) for a in arrays],
        input_output_aliases={i: i for i in range(count)},
        cost_estimate=SMALL,
        name="after",
    )(*arrays, *tokens)


def split_kernel(start, place_ref, own_ref, got_ref, token_ref, *outs):
    zh, x = place_ref[0], place_ref[1]
    rows, width = outs[0].shape[0] // 2, outs[0].shape[1]
    heads = SIZES["x"]
    span = own_ref.shape[1] // (SIZES["zh"] * heads)
    for d, out in enumerate(outs):
        head = lax.rem(x + d, heads)
        here = pl.multiple_of((zh * heads + head) * span + start, 128)
        there = pl.multiple_of(head * width, 128)
        out[pl.ds(pl.multiple_of(zh * rows, 64), rows), :] = own_ref[:, pl.ds(here, width)]
        out[pl.ds(pl.multiple_of((1 - zh) * rows, 64), rows), :] = got_ref[:, pl.ds(there, width)]


def split(place, own, got, token, start, width):
    whole = pl.BlockSpec(memory_space=pltpu.VMEM)
    return pl.pallas_call(
        functools.partial(split_kernel, start),
        in_specs=[
            pl.BlockSpec(memory_space=pltpu.SMEM), whole, whole, pl.BlockSpec(memory_space=pl.ANY),
        ],
        out_specs=[whole] * SIZES["x"],
        out_shape=[jax.ShapeDtypeStruct((2 * own.shape[0], width), own.dtype)] * SIZES["x"],
        cost_estimate=SMALL,
        name="split",
    )(place, own, got, token)


def merge_kernel(place_ref, *refs):
    x = place_ref[1]
    heads = SIZES["x"]
    out_ref = refs[-1]
    rows = refs[0].shape[0] // 2
    for d in range(heads):
        source = lax.rem(x + heads - d, heads)
        for side in range(2):
            to = pl.ds(pl.multiple_of((side * heads + source) * rows, 64), rows)
            out_ref[to, :] = refs[d][side * rows : (side + 1) * rows, :]


def merge(place, blocks, *tokens):
    rows, width = blocks[0].shape
    whole = pl.BlockSpec(memory_space=pltpu.VMEM)
    return pl.pallas_call(
        merge_kernel,
        in_specs=[pl.BlockSpec(memory_space=pltpu.SMEM)]
        + [whole] * len(blocks)
        + [pl.BlockSpec(memory_space=pl.ANY)] * len(tokens),
        out_specs=whole,
        out_shape=jax.ShapeDtypeStruct((len(blocks) * rows, width), blocks[0].dtype),
        cost_estimate=SMALL,
        name="merge",
    )(place, *blocks, *tokens)


DEPTH = 4
BLOCK = 128


def project_kernel(pieces, skip, cols_ref, x_own, x_sib, *refs):
    weights = refs[:pieces]
    refs = refs[pieces + 1 :]
    before = refs[:2] if skip else (None, None)
    if skip:
        refs = refs[2:]
    outs = refs[:2]
    x_buf, w_buf, sems = refs[2:]
    copies = []
    for p in range(pieces):
        group = [pltpu.make_async_copy(weights[p], w_buf.at[p], sems.at[2 * DEPTH, p])]
        for j in range(DEPTH):
            column = pl.multiple_of(cols_ref[(p + skip) * DEPTH + j] * BLOCK, BLOCK)
            for half, source in enumerate((x_own, x_sib)):
                group.append(
                    pltpu.make_async_copy(
                        source.at[:, pl.ds(column, BLOCK)],
                        x_buf.at[half, p, :, pl.ds(j * BLOCK, BLOCK)],
                        sems.at[half * DEPTH + j, p],
                    )
                )
        for copy in group:
            copy.start()
        copies.append(group)
    for p in range(pieces):
        for copy in copies[p]:
            copy.wait()
        for half in range(2):
            term = jnp.dot(x_buf[half, p], w_buf[p], preferred_element_type=jnp.float32)
            if p == 0:
                outs[half][...] = before[half][...] + term if skip else term
            else:
                outs[half][...] += term


def project(cols, x_own, x_sib, weights, token, before=(), skip=0):
    rows = x_own.shape[0]
    depth, width = weights[0].shape
    pieces = len(weights)
    out = jax.ShapeDtypeStruct((rows, width), jnp.float32)
    return pl.pallas_call(
        functools.partial(project_kernel, pieces, skip),
        in_specs=[pl.BlockSpec(memory_space=pltpu.SMEM)]
        + [pl.BlockSpec(memory_space=pl.ANY)] * (3 + pieces)
        + [pl.BlockSpec(memory_space=pltpu.VMEM)] * len(before),
        out_specs=[pl.BlockSpec(memory_space=pltpu.VMEM)] * 2,
        out_shape=[out, out],
        scratch_shapes=[
            pltpu.VMEM((2, pieces, rows, depth), jnp.bfloat16),
            pltpu.VMEM((pieces, depth, width), jnp.bfloat16),
            pltpu.SemaphoreType.DMA((2 * DEPTH + 1, pieces)),
        ],
        compiler_params=pltpu.CompilerParams(vmem_limit_bytes=56 * MIB),
        cost_estimate=SMALL,
        name="project",
    )(cols, x_own, x_sib, *weights, token, *before)


def turn_kernel(turned, scale, mine_ref, other_ref, bias_ref, cos_ref, sin_ref, order_ref, *refs):
    out_ref = refs[-1]
    rows = mine_ref.shape[0]
    both = mine_ref[...] + other_ref[...] + bias_ref[...]
    cosine, sine = cos_ref[...], sin_ref[...]
    half = HEAD_DIM // 2
    heads = []
    for head in range(both.shape[1] // HEAD_DIM):
        x = both[:, head * HEAD_DIM : (head + 1) * HEAD_DIM]
        if head < turned:
            swapped = jnp.concatenate([x[:, half:], x[:, :half]], axis=1)
            x = (x * cosine + swapped * sine) * scale
        heads.append(x.astype(out_ref.dtype))
    out_ref[:rows] = jnp.dot(
        order_ref[...], jnp.concatenate(heads, axis=1), preferred_element_type=jnp.float32
    ).astype(out_ref.dtype)
    if len(refs) > 1:
        out_ref[rows:] = refs[0][...]


def turn(turned, scale, mine, other, bias, cosine, sine, order, below=()):
    rows, width = mine.shape
    extra = sum(b.shape[0] for b in below)
    return pl.pallas_call(
        functools.partial(turn_kernel, turned, scale),
        out_shape=jax.ShapeDtypeStruct((rows + extra, width), jnp.bfloat16),
        cost_estimate=SMALL,
        name="turn",
    )(mine, other, bias, cosine, sine, order, *below)


STRIP = 128
TAKE = 128
KV_PIECES = 2 * PIECES
KEY_TILE = TAKE * KV_PIECES
SUMS = 16


UNDER = 16


def attend_kernel(top_ref, q_ref, qpos_ref, back_ref, *refs):
    pieces = refs[:KV_PIECES]
    out_ref, gathered, v_ref, k_ref, low_ref = refs[KV_PIECES:]
    size = q_ref.shape[0] * pl.num_programs(0)
    tiles = size // TAKE
    width = QPG * STRIP
    i = pl.program_id(0)

    @pl.when(i == 0)
    def _():
        under = [p[size : size + UNDER, :].astype(jnp.float32) for p in pieces]
        for t in range(tiles):
            rows = slice(t * TAKE, (t + 1) * TAKE)
            values = jnp.concatenate([p[rows, HEAD_DIM:] for p in pieces], axis=0)
            v_ref[t, :HEAD_DIM] = values.T
            v_ref[t, HEAD_DIM:] = jnp.ones((SUMS, KEY_TILE), jnp.bfloat16)
            row, lanes = t // 2, slice(t % 2 * TAKE, (t % 2 + 1) * TAKE)
            place = jnp.concatenate(
                [u[row : row + 1, lanes] * 128.0 + u[row + 2 : row + 3, lanes] for u in under],
                axis=0,
            )
            low_ref[t] = jnp.min(place).astype(jnp.int32)
            place = place.T
            for c in range(KV_PIECES):
                k_ref[t, c * TAKE : (c + 1) * TAKE] = jnp.broadcast_to(
                    place[:, c : c + 1], (TAKE, STRIP)
                )

    needed = jnp.int32(0)
    for t in range(tiles):
        needed += (low_ref[t] <= top_ref[i]).astype(jnp.int32)
    q = jnp.concatenate(
        [q_ref[:, h * HEAD_DIM : (h + 1) * HEAD_DIM] for h in range(QPG)], axis=0
    ).T
    qpos = qpos_ref[0]

    def absorb(t, state):
        best, accum = state
        rows = pl.ds(pl.multiple_of(t * TAKE, TAKE), TAKE)
        keys = jnp.concatenate([p[rows, :HEAD_DIM] for p in pieces], axis=0)
        score = jnp.dot(keys, q, preferred_element_type=jnp.float32)
        allowed = k_ref[t] <= qpos
        score = jnp.concatenate(
            [
                jnp.where(allowed, score[:, h * STRIP : (h + 1) * STRIP], -1e30)
                for h in range(QPG)
            ],
            axis=1,
        )
        newest = jnp.maximum(best, jnp.max(score, axis=0, keepdims=True))
        prob = jnp.exp2((score - newest).astype(jnp.bfloat16))
        accum = accum * jnp.exp2(best - newest) + jnp.dot(
            v_ref[t], prob, preferred_element_type=jnp.float32
        )
        return newest, accum

    state = (
        jnp.full((1, width), -1e30, jnp.float32),
        jnp.zeros((HEAD_DIM + SUMS, width), jnp.float32),
    )
    _, accum = lax.fori_loop(0, needed, absorb, state)
    result = (accum[:HEAD_DIM] / accum[HEAD_DIM : HEAD_DIM + 1]).T.astype(jnp.bfloat16)
    rows = pl.ds(pl.multiple_of(i * STRIP, STRIP), STRIP)
    for h in range(QPG):
        gathered[rows, h * HEAD_DIM : (h + 1) * HEAD_DIM] = result[h * STRIP : (h + 1) * STRIP]

    @pl.when(i == pl.num_programs(0) - 1)
    def _():
        out_ref[...] = jnp.dot(
            back_ref[...], gathered[...], preferred_element_type=jnp.float32
        ).astype(out_ref.dtype)


def attend(q, place, back, pieces):
    rows, width = q.shape
    strips, tiles = rows // STRIP, rows // TAKE
    qpos = place.reshape(strips, 1, STRIP)
    return pl.pallas_call(
        attend_kernel,
        grid_spec=pltpu.PrefetchScalarGridSpec(
            num_scalar_prefetch=1,
            grid=(strips,),
            in_specs=[
                pl.BlockSpec((STRIP, width), lambda i, *_: (i, 0)),
                pl.BlockSpec((1, 1, STRIP), lambda i, *_: (i, 0, 0)),
                pl.BlockSpec((rows, rows), lambda i, *_: (0, 0)),
            ]
            + [pl.BlockSpec((rows + UNDER, 2 * HEAD_DIM), lambda i, *_: (0, 0))] * KV_PIECES,
            out_specs=pl.BlockSpec((rows, width), lambda i, *_: (0, 0)),
            scratch_shapes=[
                pltpu.VMEM((rows, width), jnp.bfloat16),
                pltpu.VMEM((tiles, HEAD_DIM + SUMS, KEY_TILE), jnp.bfloat16),
                pltpu.VMEM((tiles, KEY_TILE, STRIP), jnp.float32),
                pltpu.SMEM((tiles,), jnp.int32),
            ],
        ),
        out_shape=jax.ShapeDtypeStruct((rows, width), jnp.bfloat16),
        compiler_params=pltpu.CompilerParams(vmem_limit_bytes=56 * MIB),
        cost_estimate=SMALL,
        name="attend",
    )(qpos[:, 0, -1], q, qpos.astype(jnp.float32), back, *pieces)


def angles(positions, width):
    half = width // 2
    freq = jnp.exp(jnp.arange(half, dtype=jnp.float32) * (-2.0 * math.log(theta_base) / width))
    phase = positions.astype(jnp.float32)[:, None] * freq[None, :]
    return (jnp.cos(phase), jnp.sin(phase))


def local(tokens, positions, stored_qkv, block_order, qkv_bias):
    rows = tokens.shape[0]
    zl, y, core = (lax.axis_index(a) for a in CTX)
    zh, x = (lax.axis_index(a) for a in HEAD)
    wide = QPG * HEAD_DIM
    half = PIECES // 2

    at = jnp.stack([zh, x]).astype(jnp.int32)
    span = stored_qkv.shape[1] // (SIZES["zh"] * SIZES["x"])
    heads = SIZES["x"]

    def give(start, width):
        cut = [
            lax.dynamic_slice_in_dim(stored_qkv, ((1 - zh) * heads + j) * span + start, width, axis=1)
            for j in range(heads)
        ]
        return jnp.concatenate(cut, axis=1)

    def along_x(parts):
        return [shift(p, "x", d) if d else p for d, p in enumerate(parts)]

    got_kv = shift(give(wide, span - wide), "zh", 1)
    got_q = shift(give(0, wide), "zh", 1)
    x_sib = shift(tokens, "core", 1)
    leaving_kv = split(at, stored_qkv, got_kv, got_kv, wide, span - wide)
    leaving_q = split(at, stored_qkv, got_q, leaving_kv[1], 0, wide)
    weight_kv = merge(at, along_x(leaving_kv), x_sib)
    weight_q = merge(at, along_x(leaving_q), weight_kv)

    rank = jnp.sum(positions[None, :] < positions[:, None], axis=1, dtype=jnp.int32)
    chosen = rank[None, :] == jnp.arange(rows, dtype=jnp.int32)[:, None]
    order = chosen.astype(jnp.bfloat16)
    back = (rank[:, None] == jnp.arange(rows, dtype=jnp.int32)[None, :]).astype(jnp.bfloat16)
    place = jnp.sum(jnp.where(chosen, positions[None, :], 0), axis=1, dtype=jnp.int32)

    place_rows = jnp.concatenate([place // 128, place % 128]).reshape(-1, 2 * HEAD_DIM)
    below = jnp.pad(place_rows, ((0, UNDER - place_rows.shape[0]), (0, 0))).astype(jnp.bfloat16)

    owners = jnp.stack([(((zl + a) % 2) * 4 + (y + b) % 4) * 2 + core for a, b in OFFSETS])
    blocks = owners[:, None] * DEPTH + jnp.arange(DEPTH, dtype=jnp.int32)[None, :]
    cols = block_order[blocks.reshape(-1)]

    cosine, sine = angles(positions, HEAD_DIM)
    cosine, sine = jnp.concatenate([cosine, cosine], axis=1), jnp.concatenate([-sine, sine], axis=1)

    scale = math.log2(math.e) / math.sqrt(HEAD_DIM)

    def start(block):
        return shift(block, "zl", 1), shift(block, "y", 1), shift(block, "y", -1)

    over, left, right = start(weight_kv)
    far = shift(weight_kv, "y", 2)
    over, far, weight_q = after([over, far, weight_q], left, right)
    near_kv = [weight_kv, over, left, right]
    late_kv = second(over, far)
    sums = project(cols, tokens, x_sib, near_kv, over)
    over, left, right = start(weight_q)
    far = shift(weight_q, "y", 2)
    own, away = project(cols, tokens, x_sib, late_kv, sums[0], sums, half)
    kv = turn(1, 1.0, own, shift(away, "core", 1), qkv_bias[None, wide:], cosine, sine, order, [below])
    over, far, kv = after([over, far, kv], left, right)
    near_q = [weight_q, over, left, right]
    late_q = second(over, far)
    over, left, right = start(kv)
    sums = project(cols, tokens, x_sib, near_q, kv)
    kv, over = after([kv, over], left, right, *late_q, sums[0])
    near = [kv, over, left, right]
    late = [shift(kv, "y", 2), shift(over, "y", 1), shift(over, "y", -1), shift(over, "y", 2)]
    own, away = project(cols, tokens, x_sib, late_q, over, sums, half)
    *pieces, away = after([*near, *late, away], own)
    pieces += [shift(b, "core", 1) for b in pieces]
    q = turn(QPG, scale, own, shift(away, "core", 1), qkv_bias[None, :wide], cosine, sine, order)
    return attend(q, place, back, pieces)


def solution(mesh):
    fine = Mesh(mesh.devices.reshape(tuple(SIZES.values())), tuple(SIZES))
    placed = (P(CTX, None), P(CTX), P(CTX + HEAD, None), P(), P(HEAD))
    return jax.shard_map(
        local, mesh=fine, in_specs=placed, out_specs=P(CTX, HEAD), check_vma=False
    )
```
